1024 devices in a mesh: blk: 128 (over y, z), rep: 8 (over x, core).
Axes of the slice: x: 4, y: 8, z: 16, core: 2. Of those that a mesh axis runs over, the one named last changes fastest.
Arguments:
- features: bfloat16 [65536, 128], P('blk'), may hold values from -6 to 6
- band_weight: bfloat16 [65536, 16384], P('blk', 'rep'), may hold values from -0.03125 to 0.03125
- far_weight: bfloat16 [65536, 2048], P('blk', 'rep'), may hold values from -0.09375 to 0.09375
- send_rows: int32 [128, 8, 256], P('blk', 'rep'), may hold values from 0 to 511
- layer_one: bfloat16 [128, 256], replicated, may hold values from -0.5 to 0.5
- layer_two: bfloat16 [256, 128], replicated, may hold values from -0.375 to 0.375
- cotangent: bfloat16 [65536, 128], P('blk'), may hold values from -0.0234375 to 0.0234375
Outputs:
- scores: bfloat16 [65536, 128], P('blk')
- weight_grad: float32 [256, 128], replicated
The draws below stay inside these ranges and needn't reach their ends.
All inputs are finite; a program needn't handle non-finite values.
Results may differ from the reference program's by a relative error of at most 0.0058.
Values may be sent and summed in bfloat16 or wider, within the bound.
A program may use at most 32 MiB of HBM per device.

```python
import jax
import jax.numpy as jnp
from jax import lax

FEAT = 128
HID = 256
CLASSES = 128
ROWS = 512
CAP = 2
STEPS = 4
NODES = 65536
N_BLK = 128
N_REP = 8


def place_ends(entries, stream_key, low, high):
    longest = entries.shape.index(max(entries.shape))
    spots = []
    for shift in (0, 1):
        where = [jax.random.randint(jax.random.fold_in(stream_key, axis), (), 0, length) for axis, length in enumerate(entries.shape)]
        where[longest] = (where[longest] + shift) % entries.shape[longest]
        spots.append(tuple(where))
    return entries.at[spots[0]].set(low).at[spots[1]].set(high)


def level_of(stream_key, shape, pieces, smallest, top_value):
    def one(dim, blocks):
        steps = jax.random.uniform(jax.random.fold_in(jax.random.fold_in(stream_key, 6), dim), (blocks,), jnp.float32, smallest / len(pieces), top_value / len(pieces))
        return jnp.repeat(jnp.exp(steps), shape[dim] // blocks).reshape((-1,) + (1,) * (len(shape) - dim - 1))

    level = one(*pieces[0])
    for cut in pieces[1:]:
        level = level * one(*cut)
    return level


def centred(rng, shape, scale, reach, split=(), kind=jnp.bfloat16):
    drawn = scale * jax.random.normal(rng, shape, jnp.float32)
    if split:
        drawn = drawn * level_of(rng, shape, split, -0.22, 0.18)
    return jnp.clip(drawn, -reach, reach).astype(kind)


def setup_inputs(seed: int = 0) -> dict:
    key_list = jax.random.split(jax.random.key(seed), 8)
    features = centred(key_list[0], (NODES, FEAT), 1.0, 6.0, ((0, 128),))
    band_weight = centred(key_list[1], (NODES, N_REP * STEPS * ROWS), (2 * N_REP * STEPS * ROWS) ** -0.5, 0.03125, ((0, 128), (1, 8)))
    far_weight = centred(key_list[2], (NODES, N_REP * N_BLK * CAP), (2 * N_REP * N_BLK * CAP) ** -0.5, 0.09375, ((0, 128), (1, 8)))
    send_rows = place_ends(jax.random.randint(key_list[3], (N_BLK, N_REP, N_BLK * CAP), 0, ROWS), jax.random.fold_in(key_list[3], 1), 0, ROWS - 1).astype(jnp.int32)
    layer_one = centred(key_list[4], (FEAT, HID), FEAT ** -0.5, 0.5)
    layer_two = centred(key_list[5], (HID, CLASSES), HID ** -0.5, 0.375)
    cotangent = centred(key_list[6], (NODES, CLASSES), NODES ** -0.5, 0.0234375, ((0, 128),))
    return dict(features=features, band_weight=band_weight, far_weight=far_weight, send_rows=send_rows, layer_one=layer_one, layer_two=layer_two, cotangent=cotangent)


def aggregate(node_values, band_weight, far_weight, send_rows):
    width = node_values.shape[1]
    blocks = node_values.reshape(N_BLK, ROWS, width)
    band_count = N_REP * STEPS

    def block_sum(index):
        band_rows = lax.dynamic_slice_in_dim(band_weight, index * ROWS, ROWS, 0)
        source_index = (index - jnp.arange(band_count, dtype=jnp.int32)) % N_BLK
        sources = blocks[source_index].reshape(band_count * ROWS, width)
        summed = jnp.dot(band_rows, sources, preferred_element_type=jnp.float32)
        far_rows = lax.dynamic_slice_in_dim(far_weight, index * ROWS, ROWS, 0)
        slot_rows = lax.dynamic_slice_in_dim(send_rows, index * CAP, CAP, 2)
        slot_rows = jnp.transpose(slot_rows, (1, 0, 2)).astype(jnp.int32)
        owner = jnp.arange(N_BLK, dtype=jnp.int32)[None, :, None]
        gathered = blocks[owner, slot_rows].reshape(N_REP * N_BLK * CAP, width)
        return summed + jnp.dot(far_rows, gathered, preferred_element_type=jnp.float32)

    result = lax.map(block_sum, jnp.arange(N_BLK, dtype=jnp.int32))
    return result.reshape(NODES, width)


def reference(features, band_weight, far_weight, send_rows, layer_one, layer_two, cotangent):
    first_rounded = aggregate(features, band_weight, far_weight, send_rows).astype(jnp.bfloat16)
    hidden = jax.nn.relu(jnp.dot(first_rounded, layer_one, preferred_element_type=jnp.float32)).astype(jnp.bfloat16)
    second_sum = aggregate(hidden, band_weight, far_weight, send_rows)
    scores = jnp.dot(second_sum, layer_two.astype(jnp.float32), precision=lax.Precision.HIGHEST).astype(jnp.bfloat16)
    weight_grad = jnp.dot(second_sum.T, cotangent.astype(jnp.float32), precision=lax.Precision.HIGHEST)
    return scores, weight_grad
```

```python
import functools

import jax
import jax.numpy as jnp
from jax import lax
from jax.experimental import pallas as pl
from jax.experimental.pallas import tpu as pltpu
from jax.sharding import PartitionSpec as P

MESH = pl.DeviceIdType.MESH
BF16 = jnp.bfloat16
F32 = jnp.float32

Y, Z, R = 8, 16, 8
N = Y * Z
ROWS = 512
FEAT = 128
HID = 256
STEPS = 4
PIECE = ROWS // R
SLOTS = 2 * N
GROUPS = Y * R
SHARE = HID // GROUPS


def dot(a, b):
    return jnp.dot(a, b, preferred_element_type=F32)


def dot_rows(a, b):
    return lax.dot_general(a, b, (((0,), (0,)), ((), ())), preferred_element_type=F32)


def split(value):
    high = value.astype(BF16)
    return high, (value - high.astype(F32)).astype(BF16)


def kernel(
    feat_hbm, band_hbm, far_hbm, rows_ref, one_hbm, two_hbm, cot_hbm,
    scores_ref, grad_ref,
    feat, band, far, one, two, cot, pick, total,
    send_far, recv_far, relay, blocks, whole, cut, shares,
    grad_cut, grad_in, grad_z, grad_out, score_cut, score_in, score_own, score_all,
    load_sem, y_sem, rep_sem,
    far_send, far_recv, own_far, relay_send, relay_recv, block_send, block_recv,
    cut_send, cut_recv, whole_send, whole_recv,
    grad_send, grad_recv, z_send, z_recv, out_send, out_recv,
    sc_send, sc_recv, sa_send, sa_recv,
):
    i, r = lax.axis_index("blk"), lax.axis_index("rep")
    y, z = i // Z, lax.rem(i, Z)
    own = pl.ds(pl.multiple_of(r * PIECE, PIECE), PIECE)

    def at(index):
        return lax.rem(index + N, N)

    def remote(src, dst, send, recv, blk, rep):
        return pltpu.make_async_remote_copy(
            src_ref=src, dst_ref=dst, send_sem=send, recv_sem=recv, device_id=(blk, rep), device_id_type=MESH
        )

    def wait_in(ref, recv):
        remote(ref, ref, recv, recv, i, r).wait_recv()

    def wait_out(ref, send):
        remote(ref, ref, send, send, i, r).wait_send()

    def z_peer(d):
        return y * Z + lax.rem(z + d, Z)

    def y_peer(d):
        return lax.rem(i + d * Z, N)

    def rep_peer(d):
        return lax.rem(r + d, R)

    barrier = pltpu.get_barrier_semaphore()
    for d in range(1, Z):
        pl.semaphore_signal(barrier, inc=1, device_id=(z_peer(d), r), device_id_type=MESH)
    for d in range(1, Y):
        pl.semaphore_signal(barrier, inc=1, device_id=(y_peer(d), r), device_id_type=MESH)
    for d in range(1, R):
        pl.semaphore_signal(barrier, inc=1, device_id=(i, rep_peer(d)), device_id_type=MESH)

    loads = [
        pltpu.make_async_copy(src, dst, load_sem.at[n])
        for n, (src, dst) in enumerate(
            [(feat_hbm, feat), (band_hbm, band), (far_hbm, far), (one_hbm, one), (two_hbm, two), (cot_hbm, cot)]
        )
    ]
    for load in loads:
        load.start()
    spot = lax.broadcasted_iota(jnp.int32, (ROWS, SLOTS), 0)
    pick[...] = jnp.where(spot == rows_ref[...], 1.0, 0.0).astype(BF16)
    loads[0].wait()

    def gather(layer, source):
        rows = dot_rows(pick[...], source[...]).astype(BF16)
        send_far[layer] = rows.reshape(N, 2, FEAT)

    gather(0, feat)
    pl.semaphore_wait(barrier, Z + Y + R - 3)
    for d in range(1, Y):
        pl.semaphore_signal(y_sem, inc=1, device_id=(y_peer(d), r), device_id_type=MESH)
    pl.semaphore_wait(y_sem, Y - 1)
    for d in range(1, R):
        pl.semaphore_signal(rep_sem, inc=1, device_id=(i, rep_peer(d)), device_id_type=MESH)

    def far_start(layer):
        @pl.loop(1, N)
        def _(d):
            to = at(i + d)
            remote(
                send_far.at[layer, to], recv_far.at[layer, i], far_send.at[layer], far_recv.at[layer], to, r
            ).start()

        pltpu.make_async_copy(send_far.at[layer, i], recv_far.at[layer, i], own_far.at[layer]).start()

    def far_wait(layer):
        wait_in(recv_far.at[layer, pl.ds(0, N - 1)], far_recv.at[layer])
        pltpu.make_async_copy(send_far.at[layer, i], recv_far.at[layer, i], own_far.at[layer]).wait()
        return recv_far[layer].reshape(SLOTS, FEAT)

    def relay_start(layer, piece):
        for rep in range(1, R):
            down = rep % 4 // 2
            remote(
                piece, relay.at[layer, rep], relay_send.at[layer], relay_recv.at[layer, rep],
                at(i + 4 * rep + 3 * down), r,
            ).start()

    def relay_on(layer, piece):
        for step in range(1, STEPS):
            remote(
                piece, blocks.at[layer, step, own], block_send.at[layer], block_recv.at[layer, step], at(i + step), 0
            ).start()
        for rep in (1, 5, 2, 6, 3, 7, 4):
            down = rep % 4 // 2
            wait_in(relay.at[layer, rep], relay_recv.at[layer, rep])
            for k in range(STEPS):
                step = STEPS - 1 - k if down else k
                src, dst = relay.at[layer, rep], blocks.at[layer, step, own]
                copy = remote(
                    src, dst, block_send.at[layer], block_recv.at[layer, step], at(i - k if down else i + k), rep
                )
                if k:
                    copy.start()
                else:
                    pl.when(r != rep)(copy.start)

                    @pl.when(r == rep)
                    def _():
                        pltpu.make_async_copy(src, dst, block_recv.at[layer, step]).start()

    def own_block(layer, source):
        @pl.when(r == 0)
        def _():
            pltpu.make_async_copy(source, blocks.at[layer, 0], block_recv.at[layer, 0]).start()

    far_start(0)
    relay_start(0, feat.at[own])
    own_block(0, feat)
    pl.semaphore_wait(rep_sem, R - 1)
    relay_on(0, feat.at[own])
    for load in loads[1:]:
        load.wait()
    for step in range(STEPS):
        wait_in(blocks.at[0, step], block_recv.at[0, step])
        term = dot(band[:, step * ROWS : (step + 1) * ROWS], blocks[0, step])
        total[:, :FEAT] = term if step == 0 else total[:, :FEAT] + term
    total[:, :FEAT] += dot(far[...], far_wait(0))

    def cut_start(source, cut_ref, in_ref, send, recv):
        cut_ref[...] = source.reshape(R, PIECE, FEAT).astype(BF16)
        for d in range(1, R):
            to = rep_peer(d)
            remote(cut_ref.at[to], in_ref.at[r], send, recv, i, to).start()

    def cut_sum(own_rows, in_ref, recv):
        in_ref[r] = jnp.zeros((PIECE, FEAT), BF16)
        wait_in(in_ref.at[pl.ds(0, R - 1)], recv)
        return own_rows + jnp.sum(in_ref[...].astype(F32), axis=0)

    cut_start(total[:, :FEAT], cut, shares, cut_send, cut_recv)
    whole[own] = cut_sum(total[own, :FEAT], shares, cut_recv).astype(BF16)
    for d in range(1, R):
        remote(whole.at[own], whole.at[own], whole_send, whole_recv, i, rep_peer(d)).start()
    relay_start(1, whole.at[own])
    wait_in(whole.at[pl.ds(0, ROWS - PIECE)], whole_recv)
    gather(1, whole)
    far_start(1)
    own_block(1, whole)
    relay_on(1, whole.at[own])

    def expand(value):
        return jnp.maximum(dot(value, one[...]), 0.0).astype(BF16)

    for step in range(STEPS):
        wait_in(blocks.at[1, step], block_recv.at[1, step])
        term = dot(band[:, step * ROWS : (step + 1) * ROWS], expand(blocks[1, step]))
        total[...] = term if step == 0 else total[...] + term
    total[...] += dot(far[...], expand(far_wait(1)))
    high, low = split(total[...])

    local = dot_rows(high, cot[...]) + dot_rows(low, cot[...])
    grad_cut[...] = local.reshape(GROUPS, SHARE, FEAT).astype(BF16)
    mine = y * R + r

    def group_loop(body):
        @pl.loop(1, GROUPS)
        def _(d):
            to_y, to_r = lax.rem(y + d // R, Y), lax.rem(r + lax.rem(d, R), R)
            body(to_y * R + to_r, to_y * Z + z, to_r)

    def grad_go(slot, blk, rep):
        remote(grad_cut.at[slot], grad_in.at[mine], grad_send, grad_recv, blk, rep).start()

    group_loop(grad_go)

    part = dot(high, two[...]) + dot(low, two[...])
    score_own[...] = part.reshape(R, PIECE, FEAT)
    cut_start(part, score_cut, score_in, sc_send, sc_recv)

    grad_in[mine] = grad_cut[mine]
    wait_in(grad_in.at[pl.ds(0, GROUPS - 1)], grad_recv)
    grad_z[z] = jnp.sum(grad_in[...].astype(F32), axis=0)
    for d in range(1, Z):
        remote(grad_z.at[z], grad_z.at[z], z_send, z_recv, z_peer(d), r).start()

    score_all[own] = cut_sum(score_own[r], score_in, sc_recv).astype(BF16)
    for d in range(1, R):
        remote(score_all.at[own], score_all.at[own], sa_send, sa_recv, i, rep_peer(d)).start()

    wait_in(grad_z.at[pl.ds(0, Z - 1)], z_recv)
    grad_out[mine] = jnp.sum(grad_z[...], axis=0).astype(BF16)

    def out_go(slot, blk, rep):
        remote(grad_out.at[mine], grad_out.at[mine], out_send, out_recv, blk, rep).start()

    group_loop(out_go)
    wait_in(score_all.at[pl.ds(0, ROWS - PIECE)], sa_recv)
    scores_ref[...] = score_all[...]
    wait_in(grad_out.at[pl.ds(0, GROUPS - 1)], out_recv)
    grad_ref[...] = grad_out[...].astype(F32).reshape(HID, FEAT)

    for layer in range(2):
        wait_out(recv_far.at[layer, pl.ds(0, N - 1)], far_send.at[layer])
        wait_out(relay.at[layer, pl.ds(1, R - 1)], relay_send.at[layer])
        wait_out(relay.at[layer, pl.ds(1, 3)], block_send.at[layer])
        for k in range(STEPS - 1):
            wait_out(relay.at[layer, pl.ds(1, R - 1)], block_send.at[layer])
        wait_out(relay.at[layer, pl.ds(1, R - 2)], block_send.at[layer])
        pl.when(r == 0)(lambda: wait_out(relay.at[layer, 1], block_send.at[layer]))
    wait_out(shares.at[pl.ds(0, R - 1)], cut_send)
    wait_out(whole.at[pl.ds(0, ROWS - PIECE)], whole_send)
    wait_out(score_in.at[pl.ds(0, R - 1)], sc_send)
    wait_out(score_all.at[pl.ds(0, ROWS - PIECE)], sa_send)
    wait_out(grad_in.at[pl.ds(0, GROUPS - 1)], grad_send)
    wait_out(grad_z.at[pl.ds(0, Z - 1)], z_send)
    wait_out(grad_out.at[pl.ds(0, GROUPS - 1)], out_send)


def per_device(features, band_weight, far_weight, send_rows, layer_one, layer_two, cotangent):
    dma, regular, vmem = pltpu.SemaphoreType.DMA, pltpu.SemaphoreType.REGULAR, pltpu.VMEM
    anywhere = pl.BlockSpec(memory_space=pl.ANY)
    here = pl.BlockSpec(memory_space=pltpu.VMEM)
    scratch = [
        vmem((ROWS, FEAT), BF16),
        vmem((ROWS, STEPS * ROWS), BF16),
        vmem((ROWS, SLOTS), BF16),
        vmem((FEAT, HID), BF16),
        vmem((HID, FEAT), BF16),
        vmem((ROWS, FEAT), BF16),
        vmem((ROWS, SLOTS), BF16),
        vmem((ROWS, HID), F32),
        vmem((2, N, 2, FEAT), BF16),
        vmem((2, N, 2, FEAT), BF16),
        vmem((2, R, PIECE, FEAT), BF16),
        vmem((2, STEPS, ROWS, FEAT), BF16),
        vmem((ROWS, FEAT), BF16),
        vmem((R, PIECE, FEAT), BF16),
        vmem((R, PIECE, FEAT), BF16),
        vmem((GROUPS, SHARE, FEAT), BF16),
        vmem((GROUPS, SHARE, FEAT), BF16),
        vmem((Z, SHARE, FEAT), F32),
        vmem((GROUPS, SHARE, FEAT), BF16),
        vmem((R, PIECE, FEAT), BF16),
        vmem((R, PIECE, FEAT), BF16),
        vmem((R, PIECE, FEAT), F32),
        vmem((ROWS, FEAT), BF16),
        dma((6,)), regular, regular,
        dma((2,)), dma((2,)), dma((2,)), dma((2,)), dma((2, R)), dma((2,)), dma((2, STEPS)),
        dma, dma, dma, dma,
        dma, dma, dma, dma, dma, dma,
        dma, dma, dma, dma,
    ]
    return pl.pallas_call(
        kernel,
        out_shape=(jax.ShapeDtypeStruct((ROWS, FEAT), BF16), jax.ShapeDtypeStruct((HID, FEAT), F32)),
        in_specs=[anywhere, anywhere, anywhere, here, anywhere, anywhere, anywhere],
        out_specs=(here, here),
        scratch_shapes=scratch,
        name="graph",
        compiler_params=pltpu.CompilerParams(collective_id=0, has_side_effects=True, vmem_limit_bytes=60 << 20),
    )(features, band_weight, far_weight, send_rows.reshape(1, SLOTS), layer_one, layer_two, cotangent)


def solution(mesh):
    return jax.shard_map(
        per_device,
        mesh=mesh,
        in_specs=(
            P("blk", None),
            P("blk", "rep"),
            P("blk", "rep"),
            P("blk", "rep", None),
            P(),
            P(),
            P("blk", None),
        ),
        out_specs=(P("blk", None), P()),
        check_vma=False,
    )
```

```python
import functools

import jax
import jax.numpy as jnp
from jax import lax
from jax.experimental import pallas as pl
from jax.experimental.pallas import tpu as pltpu
from jax.sharding import PartitionSpec as P

MESH = pl.DeviceIdType.MESH
BF16 = jnp.bfloat16
F32 = jnp.float32

Y, Z, R = 8, 16, 8
N = Y * Z
ROWS = 512
FEAT = 128
HID = 256
STEPS = 4
PIECE = ROWS // R
SLOTS = 2 * N
GROUPS = Y * R
SHARE = HID // GROUPS
CENTRES = (4, 13, 20, 29, 7, 10, 23, 26)
STRAIGHT = (31, 18, 17, 15, 16, 2, 1)


def far_first(n, size):
    half = (n + 1) // 2
    return size // 2 + half * (1 - 2 * (n % 2))


def dot(a, b):
    return jnp.dot(a, b, preferred_element_type=F32)


def dot_rows(a, b):
    return lax.dot_general(a, b, (((0,), (0,)), ((), ())), preferred_element_type=F32)


def split(value):
    high = value.astype(BF16)
    return high, (value - high.astype(F32)).astype(BF16)


def kernel(
    feat_hbm, band_hbm, far_hbm, rows_ref, one_hbm, two_hbm, cot_hbm,
    scores_hbm, grad_hbm,
    feat, band, far, one, two, cot, pick, total, pulled, pulled_far, local, grad_full,
    send_far, recv_far, relay, blocks, whole, cut, shares,
    grad_cut, grad_in, grad_z, grad_out, score_cut, score_in, score_own, score_all,
    load_sem, save_sem, y_sem, rep_sem,
    far_send, far_recv, own_far, relay_send, relay_recv, block_send, block_recv,
    cut_send, cut_recv, whole_send, whole_recv,
    grad_send, grad_recv, z_send, z_recv, out_send, out_recv,
    sc_send, sc_recv, sa_send, sa_recv,
):
    i, r = lax.axis_index("blk"), lax.axis_index("rep")
    y, z = i // Z, lax.rem(i, Z)
    own = pl.ds(pl.multiple_of(r * PIECE, PIECE), PIECE)

    def at(index):
        return lax.rem(index + N, N)

    def remote(src, dst, send, recv, blk, rep):
        return pltpu.make_async_remote_copy(
            src_ref=src, dst_ref=dst, send_sem=send, recv_sem=recv, device_id=(blk, rep), device_id_type=MESH
        )

    def wait_in(ref, recv):
        remote(ref, ref, recv, recv, i, r).wait_recv()

    def wait_out(ref, send):
        remote(ref, ref, send, send, i, r).wait_send()

    def z_peer(d):
        return y * Z + lax.rem(z + d, Z)

    def y_peer(d):
        return lax.rem(i + d * Z, N)

    def rep_peer(d):
        return lax.rem(r + d, R)

    z_order, y_order, rep_order = ([far_first(n, size) for n in range(size - 1)] for size in (Z, Y, R))

    barrier = pltpu.get_barrier_semaphore()
    for d in z_order:
        pl.semaphore_signal(barrier, inc=1, device_id=(z_peer(d), r), device_id_type=MESH)
    for d in y_order:
        pl.semaphore_signal(barrier, inc=1, device_id=(y_peer(d), r), device_id_type=MESH)
    for d in rep_order:
        pl.semaphore_signal(barrier, inc=1, device_id=(i, rep_peer(d)), device_id_type=MESH)

    loads = [
        pltpu.make_async_copy(src, dst, load_sem.at[n])
        for n, (src, dst) in enumerate(
            [(feat_hbm, feat), (band_hbm, band), (far_hbm, far), (one_hbm, one), (two_hbm, two), (cot_hbm, cot)]
        )
    ]
    for load in loads:
        load.start()
    spot = lax.broadcasted_iota(jnp.int32, (ROWS, SLOTS), 0)
    pick[...] = jnp.where(spot == rows_ref[...], 1.0, 0.0).T.astype(BF16)
    loads[0].wait()

    def gather(layer, source):
        rows = dot(pick[...], source[...]).astype(BF16)
        send_far[layer] = rows.reshape(N, 2, FEAT)

    def pair(ref, value):
        ref[:, :FEAT], ref[:, FEAT:] = split(value)

    gather(0, feat)
    pl.semaphore_wait(barrier, Z + Y + R - 3)
    for d in y_order:
        pl.semaphore_signal(y_sem, inc=1, device_id=(y_peer(d), r), device_id_type=MESH)
    pl.semaphore_wait(y_sem, Y - 1)
    for d in rep_order:
        pl.semaphore_signal(rep_sem, inc=1, device_id=(i, rep_peer(d)), device_id_type=MESH)

    def far_start(layer, low, high):
        @pl.loop(low, high)
        def _(n):
            to_y = lax.rem(y + far_first(lax.rem(n, Y), Y), Y)
            to = to_y * Z + lax.rem(z + far_first(n // Y, Z), Z)
            remote(
                send_far.at[layer, to], recv_far.at[layer, i], far_send.at[layer], far_recv.at[layer], to, r
            ).start()

    def far_own(layer):
        pltpu.make_async_copy(send_far.at[layer, i], recv_far.at[layer, i], own_far.at[layer]).start()

    def far_wait(layer):
        wait_in(recv_far.at[layer, pl.ds(0, N - 1)], far_recv.at[layer])
        pltpu.make_async_copy(send_far.at[layer, i], recv_far.at[layer, i], own_far.at[layer]).wait()
        return recv_far[layer].reshape(SLOTS, FEAT)

    def hand(layer, slot, piece, back):
        remote(
            piece, relay.at[layer, slot], relay_send.at[layer], relay_recv.at[layer, slot], at(i + back), r
        ).start()

    def hand_first(layer, piece):
        for slot in (3, 1, 0, 2):
            hand(layer, slot, piece, CENTRES[slot])

    def straight(layer, piece):
        for back in STRAIGHT:
            rep, step = back // STEPS, back % STEPS
            remote(
                piece, blocks.at[layer, step, own], block_send.at[layer], block_recv.at[layer, step], at(i + back), rep
            ).start()

    def pass_on(layer, slot):
        piece = relay.at[layer, slot]
        wait_in(piece, relay_recv.at[layer, slot])
        if slot < 4:
            hand(layer, slot + 4, piece, CENTRES[slot + 4] - CENTRES[slot])
        for delta in (1, -1):
            rep, step = (CENTRES[slot] + delta) // STEPS, (CENTRES[slot] + delta) % STEPS
            remote(
                piece, blocks.at[layer, step, own], block_send.at[layer], block_recv.at[layer, step], at(i + delta), rep
            ).start()
        rep, step = CENTRES[slot] // STEPS, CENTRES[slot] % STEPS
        dst = blocks.at[layer, step, own]
        copy = remote(piece, dst, block_send.at[layer], block_recv.at[layer, step], i, rep)
        pl.when(r != rep)(copy.start)

        @pl.when(r == rep)
        def _():
            pltpu.make_async_copy(piece, dst, block_recv.at[layer, step]).start()

    def own_block(layer, source):
        @pl.when(r == 0)
        def _():
            pltpu.make_async_copy(source, blocks.at[layer, 0], block_recv.at[layer, 0]).start()

    hand_first(0, feat.at[own])
    far_start(0, 0, N // 2)
    pl.semaphore_wait(rep_sem, R - 1)
    straight(0, feat.at[own])
    for slot in (0, 2, 1, 3):
        pass_on(0, slot)
    far_start(0, N // 2, N - 1)
    far_own(0)
    own_block(0, feat)
    for slot in (4, 6, 5, 7):
        pass_on(0, slot)
    for load in loads[1:]:
        load.wait()
    for step in range(STEPS):
        pair(pulled.at[step], dot_rows(band[:, step * ROWS : (step + 1) * ROWS], cot[...]))
    pair(pulled_far, dot_rows(far[...], cot[...]))
    for step in range(STEPS):
        wait_in(blocks.at[0, step], block_recv.at[0, step])
        term = dot(band[:, step * ROWS : (step + 1) * ROWS], blocks[0, step])
        total[:, :FEAT] = term if step == 0 else total[:, :FEAT] + term
    total[:, :FEAT] += dot(far[...], far_wait(0))

    def cut_start(source, cut_ref, in_ref, send, recv):
        cut_ref[...] = source.reshape(R, PIECE, FEAT).astype(BF16)
        for d in rep_order:
            to = rep_peer(d)
            remote(cut_ref.at[to], in_ref.at[r], send, recv, i, to).start()

    def cut_sum(own_rows, in_ref, recv):
        in_ref[r] = jnp.zeros((PIECE, FEAT), BF16)
        wait_in(in_ref.at[pl.ds(0, R - 1)], recv)
        return own_rows + jnp.sum(in_ref[...].astype(F32), axis=0)

    cut_start(total[:, :FEAT], cut, shares, cut_send, cut_recv)
    whole[own] = cut_sum(total[own, :FEAT], shares, cut_recv).astype(BF16)
    for d in rep_order:
        remote(whole.at[own], whole.at[own], whole_send, whole_recv, i, rep_peer(d)).start()
    hand_first(1, whole.at[own])
    straight(1, whole.at[own])
    wait_in(whole.at[pl.ds(0, ROWS - PIECE)], whole_recv)
    gather(1, whole)
    far_start(1, 0, N // 2)
    for slot in (0, 2, 1, 3):
        pass_on(1, slot)
    far_start(1, N // 2, N - 1)
    far_own(1)
    own_block(1, whole)
    for slot in (4, 6, 5, 7):
        pass_on(1, slot)

    def expand(value):
        return jnp.maximum(dot(value, one[...]), 0.0).astype(BF16)

    for step in range(STEPS):
        wait_in(blocks.at[1, step], block_recv.at[1, step])
        nodes = expand(blocks[1, step])
        term = dot(band[:, step * ROWS : (step + 1) * ROWS], nodes)
        total[...] = term if step == 0 else total[...] + term
        term = dot_rows(nodes, pulled[step])
        local[...] = term if step == 0 else local[...] + term

    far_nodes = expand(far_wait(1))
    term = local[...] + dot_rows(far_nodes, pulled_far[...])
    grad_cut[...] = (term[:, :FEAT] + term[:, FEAT:]).reshape(GROUPS, SHARE, FEAT).astype(BF16)
    mine = y * R + r

    def group_loop(body):
        @pl.loop(0, GROUPS - 1)
        def _(n):
            to_y, to_r = lax.rem(y + far_first(n // R, Y), Y), lax.rem(r + far_first(lax.rem(n, R), R), R)
            body(to_y * R + to_r, to_y * Z + z, to_r)

    def grad_go(slot, blk, rep):
        remote(grad_cut.at[slot], grad_in.at[mine], grad_send, grad_recv, blk, rep).start()

    group_loop(grad_go)

    total[...] += dot(far[...], far_nodes)
    high, low = split(total[...])
    part = dot(high, two[...]) + dot(low, two[...])
    score_own[...] = part.reshape(R, PIECE, FEAT)
    cut_start(part, score_cut, score_in, sc_send, sc_recv)

    grad_in[mine] = grad_cut[mine]
    wait_in(grad_in.at[pl.ds(0, GROUPS - 1)], grad_recv)
    grad_z[z] = jnp.sum(grad_in[...].astype(F32), axis=0)
    for d in z_order:
        remote(grad_z.at[z], grad_z.at[z], z_send, z_recv, z_peer(d), r).start()

    score_all[own] = cut_sum(score_own[r], score_in, sc_recv).astype(BF16)
    for d in rep_order:
        remote(score_all.at[own], score_all.at[own], sa_send, sa_recv, i, rep_peer(d)).start()

    wait_in(grad_z.at[pl.ds(0, Z - 1)], z_recv)
    grad_out[mine] = jnp.sum(grad_z[...], axis=0).astype(BF16)

    def out_go(slot, blk, rep):
        remote(grad_out.at[mine], grad_out.at[mine], out_send, out_recv, blk, rep).start()

    group_loop(out_go)
    wait_in(score_all.at[pl.ds(0, ROWS - PIECE)], sa_recv)
    save_scores = pltpu.make_async_copy(score_all, scores_hbm, save_sem.at[0])
    save_scores.start()
    wait_in(grad_out.at[pl.ds(0, GROUPS - 1)], out_recv)
    grad_full[...] = grad_out[...].astype(F32).reshape(HID, FEAT)
    save_grad = pltpu.make_async_copy(grad_full, grad_hbm, save_sem.at[1])
    save_grad.start()

    for layer in range(2):
        wait_out(recv_far.at[layer, pl.ds(0, N - 1)], far_send.at[layer])
        wait_out(relay.at[layer], relay_send.at[layer])
        wait_out(blocks.at[layer, pl.ds(0, 3)], block_send.at[layer])
        wait_out(relay.at[layer, pl.ds(0, 5)], block_send.at[layer])
        twice = jnp.logical_or(r == 1, r == 5)
        never = jnp.logical_or(r == 0, r == 4)
        pl.when(jnp.logical_not(twice))(lambda: wait_out(relay.at[layer, 0], block_send.at[layer]))
        pl.when(never)(lambda: wait_out(relay.at[layer, 0], block_send.at[layer]))
    wait_out(shares.at[pl.ds(0, R - 1)], cut_send)
    wait_out(whole.at[pl.ds(0, ROWS - PIECE)], whole_send)
    wait_out(score_in.at[pl.ds(0, R - 1)], sc_send)
    wait_out(score_all.at[pl.ds(0, ROWS - PIECE)], sa_send)
    wait_out(grad_in.at[pl.ds(0, GROUPS - 1)], grad_send)
    wait_out(grad_z.at[pl.ds(0, Z - 1)], z_send)
    wait_out(grad_out.at[pl.ds(0, GROUPS - 1)], out_send)
    save_scores.wait()
    save_grad.wait()


def per_device(features, band_weight, far_weight, send_rows, layer_one, layer_two, cotangent):
    dma, regular, vmem = pltpu.SemaphoreType.DMA, pltpu.SemaphoreType.REGULAR, pltpu.VMEM
    anywhere = pl.BlockSpec(memory_space=pl.ANY)
    here = pl.BlockSpec(memory_space=pltpu.VMEM)
    scratch = [
        vmem((ROWS, FEAT), BF16),
        vmem((ROWS, STEPS * ROWS), BF16),
        vmem((ROWS, SLOTS), BF16),
        vmem((FEAT, HID), BF16),
        vmem((HID, FEAT), BF16),
        vmem((ROWS, FEAT), BF16),
        vmem((SLOTS, ROWS), BF16),
        vmem((ROWS, HID), F32),
        vmem((STEPS, ROWS, 2 * FEAT), BF16),
        vmem((SLOTS, 2 * FEAT), BF16),
        vmem((HID, 2 * FEAT), F32),
        vmem((HID, FEAT), F32),
        vmem((2, N, 2, FEAT), BF16),
        vmem((2, N, 2, FEAT), BF16),
        vmem((2, R, PIECE, FEAT), BF16),
        vmem((2, STEPS, ROWS, FEAT), BF16),
        vmem((ROWS, FEAT), BF16),
        vmem((R, PIECE, FEAT), BF16),
        vmem((R, PIECE, FEAT), BF16),
        vmem((GROUPS, SHARE, FEAT), BF16),
        vmem((GROUPS, SHARE, FEAT), BF16),
        vmem((Z, SHARE, FEAT), F32),
        vmem((GROUPS, SHARE, FEAT), BF16),
        vmem((R, PIECE, FEAT), BF16),
        vmem((R, PIECE, FEAT), BF16),
        vmem((R, PIECE, FEAT), F32),
        vmem((ROWS, FEAT), BF16),
        dma((6,)), dma((2,)), regular, regular,
        dma((2,)), dma((2,)), dma((2,)), dma((2,)), dma((2, R)), dma((2,)), dma((2, STEPS)),
        dma, dma, dma, dma,
        dma, dma, dma, dma, dma, dma,
        dma, dma, dma, dma,
    ]
    return pl.pallas_call(
        kernel,
        out_shape=(jax.ShapeDtypeStruct((ROWS, FEAT), BF16), jax.ShapeDtypeStruct((HID, FEAT), F32)),
        in_specs=[anywhere, anywhere, anywhere, here, anywhere, anywhere, anywhere],
        out_specs=(anywhere, anywhere),
        scratch_shapes=scratch,
        name="graph",
        compiler_params=pltpu.CompilerParams(collective_id=0, has_side_effects=True, vmem_limit_bytes=60 << 20),
    )(features, band_weight, far_weight, send_rows.reshape(1, SLOTS), layer_one, layer_two, cotangent)


def solution(mesh):
    return jax.shard_map(
        per_device,
        mesh=mesh,
        in_specs=(
            P("blk", None),
            P("blk", "rep"),
            P("blk", "rep"),
            P("blk", "rep", None),
            P(),
            P(),
            P("blk", None),
        ),
        out_specs=(P("blk", None), P()),
        check_vma=False,
    )
```

```python
import functools

import jax
import jax.numpy as jnp
from jax import lax
from jax.experimental import pallas as pl
from jax.experimental.pallas import tpu as pltpu
from jax.sharding import PartitionSpec as P

MESH = pl.DeviceIdType.MESH
BF16 = jnp.bfloat16
F32 = jnp.float32

Y, Z, R = 8, 16, 8
N = Y * Z
ROWS = 512
FEAT = 128
HID = 256
STEPS = 4
PIECE = ROWS // R
SLOTS = 2 * N
GROUPS = Y * R
SHARE = HID // GROUPS
CENTRES = (4, 13, 20, 29, 7, 10, 23, 26)
STRAIGHT = (31, 18, 17, 15, 16, 2, 1)


def far_first(n, size):
    half = (n + 1) // 2
    return size // 2 + half * (1 - 2 * (n % 2))


def dot(a, b):
    return jnp.dot(a, b, preferred_element_type=F32)


def dot_rows(a, b):
    return lax.dot_general(a, b, (((0,), (0,)), ((), ())), preferred_element_type=F32)


def split(value):
    high = value.astype(BF16)
    return high, (value - high.astype(F32)).astype(BF16)


def kernel(
    feat_hbm, band_hbm, far_hbm, rows_ref, one_hbm, two_hbm, cot_hbm,
    scores_hbm, grad_hbm,
    feat, band, far, one, two, cot, pick, total, pulled, pulled_far, local, grad_full,
    send_far, recv_far, relay, blocks, whole, cut, shares,
    grad_cut, grad_in, grad_z, grad_out, score_cut, score_in, score_own, score_all,
    load_sem, save_sem, y_sem, rep_sem,
    far_send, far_recv, own_far, relay_send, relay_recv, block_send, block_recv,
    cut_send, cut_recv, whole_send, whole_recv,
    grad_send, grad_recv, z_send, z_recv, out_send, out_recv,
    sc_send, sc_recv, sa_send, sa_recv,
):
    i, r = lax.axis_index("blk"), lax.axis_index("rep")
    y, z = i // Z, lax.rem(i, Z)
    own = pl.ds(pl.multiple_of(r * PIECE, PIECE), PIECE)

    def at(index):
        return lax.rem(index + N, N)

    def remote(src, dst, send, recv, blk, rep):
        return pltpu.make_async_remote_copy(
            src_ref=src, dst_ref=dst, send_sem=send, recv_sem=recv, device_id=(blk, rep), device_id_type=MESH
        )

    def wait_in(ref, recv):
        remote(ref, ref, recv, recv, i, r).wait_recv()

    def wait_out(ref, send):
        remote(ref, ref, send, send, i, r).wait_send()

    def z_peer(d):
        return y * Z + lax.rem(z + d, Z)

    def y_peer(d):
        return lax.rem(i + d * Z, N)

    def rep_peer(d):
        return lax.rem(r + d, R)

    z_order, y_order, rep_order = ([far_first(n, size) for n in range(size - 1)] for size in (Z, Y, R))

    barrier = pltpu.get_barrier_semaphore()
    for d in z_order:
        pl.semaphore_signal(barrier, inc=1, device_id=(z_peer(d), r), device_id_type=MESH)
    for d in y_order:
        pl.semaphore_signal(barrier, inc=1, device_id=(y_peer(d), r), device_id_type=MESH)
    for d in rep_order:
        pl.semaphore_signal(barrier, inc=1, device_id=(i, rep_peer(d)), device_id_type=MESH)

    loads = [
        pltpu.make_async_copy(src, dst, load_sem.at[n])
        for n, (src, dst) in enumerate(
            [(feat_hbm, feat), (band_hbm, band), (far_hbm, far), (one_hbm, one), (two_hbm, two), (cot_hbm, cot)]
        )
    ]
    for load in loads:
        load.start()
    spot = lax.broadcasted_iota(jnp.int32, (ROWS, SLOTS), 0)
    pick[...] = jnp.where(spot == rows_ref[...], 1.0, 0.0).T.astype(BF16)
    loads[0].wait()

    def gather(layer, source):
        rows = dot(pick[...], source[...]).astype(BF16)
        send_far[layer] = rows.reshape(N, 2, FEAT)

    def pair(ref, value):
        ref[:, :FEAT], ref[:, FEAT:] = split(value)

    gather(0, feat)
    pl.semaphore_wait(barrier, Z + Y + R - 3)
    for d in y_order:
        pl.semaphore_signal(y_sem, inc=1, device_id=(y_peer(d), r), device_id_type=MESH)
    pl.semaphore_wait(y_sem, Y - 1)

    def far_start(layer, low, high):
        @pl.loop(low, high)
        def _(n):
            to_y = lax.rem(y + far_first(lax.rem(n, Y), Y), Y)
            to = to_y * Z + lax.rem(z + far_first(n // Y, Z), Z)
            remote(
                send_far.at[layer, to], recv_far.at[layer, i], far_send.at[layer], far_recv.at[layer], to, r
            ).start()

    def far_own(layer):
        pltpu.make_async_copy(send_far.at[layer, i], recv_far.at[layer, i], own_far.at[layer]).start()

    def far_wait(layer):
        wait_in(recv_far.at[layer, pl.ds(0, N - 1)], far_recv.at[layer])
        pltpu.make_async_copy(send_far.at[layer, i], recv_far.at[layer, i], own_far.at[layer]).wait()
        return recv_far[layer].reshape(SLOTS, FEAT)

    def hand(layer, slot, piece, back):
        remote(
            piece, relay.at[layer, slot], relay_send.at[layer], relay_recv.at[layer, slot], at(i + back), r
        ).start()

    def hand_first(layer, piece):
        for slot in (3, 1, 0, 2):
            hand(layer, slot, piece, CENTRES[slot])

    def straight(layer, piece):
        for back in STRAIGHT:
            rep, step = back // STEPS, back % STEPS
            remote(
                piece, blocks.at[layer, step, own], block_send.at[layer], block_recv.at[layer, step], at(i + back), rep
            ).start()

    def pass_on(layer, slot):
        piece = relay.at[layer, slot]
        wait_in(piece, relay_recv.at[layer, slot])
        if slot < 4:
            hand(layer, slot + 4, piece, CENTRES[slot + 4] - CENTRES[slot])
        for delta in (1, -1):
            rep, step = (CENTRES[slot] + delta) // STEPS, (CENTRES[slot] + delta) % STEPS
            remote(
                piece, blocks.at[layer, step, own], block_send.at[layer], block_recv.at[layer, step], at(i + delta), rep
            ).start()
        rep, step = CENTRES[slot] // STEPS, CENTRES[slot] % STEPS
        dst = blocks.at[layer, step, own]
        copy = remote(piece, dst, block_send.at[layer], block_recv.at[layer, step], i, rep)
        pl.when(r != rep)(copy.start)

        @pl.when(r == rep)
        def _():
            pltpu.make_async_copy(piece, dst, block_recv.at[layer, step]).start()

    def own_block(layer, source):
        @pl.when(r == 0)
        def _():
            pltpu.make_async_copy(source, blocks.at[layer, 0], block_recv.at[layer, 0]).start()

    hand_first(0, feat.at[own])
    for d in rep_order:
        pl.semaphore_signal(rep_sem, inc=1, device_id=(i, rep_peer(d)), device_id_type=MESH)
    far_start(0, 0, N // 2)
    pl.semaphore_wait(rep_sem, R - 1)
    straight(0, feat.at[own])
    for slot in (0, 2, 1, 3):
        pass_on(0, slot)
    far_start(0, N // 2, N - 1)
    far_own(0)
    own_block(0, feat)
    for slot in (4, 6, 5, 7):
        pass_on(0, slot)
    for load in loads[1:]:
        load.wait()
    for step in range(STEPS):
        pair(pulled.at[step], dot_rows(band[:, step * ROWS : (step + 1) * ROWS], cot[...]))
    pair(pulled_far, dot_rows(far[...], cot[...]))
    for step in range(STEPS):
        wait_in(blocks.at[0, step], block_recv.at[0, step])
        term = dot(band[:, step * ROWS : (step + 1) * ROWS], blocks[0, step])
        total[:, :FEAT] = term if step == 0 else total[:, :FEAT] + term
    total[:, :FEAT] += dot(far[...], far_wait(0))

    def cut_start(source, cut_ref, in_ref, send, recv):
        cut_ref[...] = source.reshape(R, PIECE, FEAT).astype(BF16)
        for d in rep_order:
            to = rep_peer(d)
            remote(cut_ref.at[to], in_ref.at[r], send, recv, i, to).start()

    def cut_sum(own_rows, in_ref, recv):
        in_ref[r] = jnp.zeros((PIECE, FEAT), BF16)
        wait_in(in_ref.at[pl.ds(0, R - 1)], recv)
        return own_rows + jnp.sum(in_ref[...].astype(F32), axis=0)

    cut_start(total[:, :FEAT], cut, shares, cut_send, cut_recv)
    whole[own] = cut_sum(total[own, :FEAT], shares, cut_recv).astype(BF16)
    for d in rep_order:
        remote(whole.at[own], whole.at[own], whole_send, whole_recv, i, rep_peer(d)).start()
    hand_first(1, whole.at[own])
    straight(1, whole.at[own])
    wait_in(whole.at[pl.ds(0, ROWS - PIECE)], whole_recv)
    gather(1, whole)
    far_start(1, 0, N // 2)
    for slot in (0, 2, 1, 3):
        pass_on(1, slot)
    far_start(1, N // 2, N - 1)
    far_own(1)
    own_block(1, whole)
    for slot in (4, 6, 5, 7):
        pass_on(1, slot)

    def expand(value):
        return jnp.maximum(dot(value, one[...]), 0.0).astype(BF16)

    for step in range(STEPS):
        wait_in(blocks.at[1, step], block_recv.at[1, step])
        nodes = expand(blocks[1, step])
        term = dot(band[:, step * ROWS : (step + 1) * ROWS], nodes)
        total[...] = term if step == 0 else total[...] + term
        term = dot_rows(nodes, pulled[step])
        local[...] = term if step == 0 else local[...] + term

    far_nodes = expand(far_wait(1))
    term = local[...] + dot_rows(far_nodes, pulled_far[...])
    grad_cut[...] = (term[:, :FEAT] + term[:, FEAT:]).reshape(GROUPS, SHARE, FEAT).astype(BF16)
    mine = y * R + r

    def group_loop(body):
        @pl.loop(0, GROUPS - 1)
        def _(n):
            to_y, to_r = lax.rem(y + far_first(n // R, Y), Y), lax.rem(r + far_first(lax.rem(n, R), R), R)
            body(to_y * R + to_r, to_y * Z + z, to_r)

    def grad_go(slot, blk, rep):
        remote(grad_cut.at[slot], grad_in.at[mine], grad_send, grad_recv, blk, rep).start()

    group_loop(grad_go)

    total[...] += dot(far[...], far_nodes)
    high, low = split(total[...])
    part = dot(high, two[...]) + dot(low, two[...])
    score_own[...] = part.reshape(R, PIECE, FEAT)
    cut_start(part, score_cut, score_in, sc_send, sc_recv)

    grad_in[mine] = grad_cut[mine]
    wait_in(grad_in.at[pl.ds(0, GROUPS - 1)], grad_recv)
    grad_z[z] = jnp.sum(grad_in[...].astype(F32), axis=0).astype(BF16)
    for d in z_order:
        remote(grad_z.at[z], grad_z.at[z], z_send, z_recv, z_peer(d), r).start()

    score_all[own] = cut_sum(score_own[r], score_in, sc_recv).astype(BF16)
    for d in rep_order:
        remote(score_all.at[own], score_all.at[own], sa_send, sa_recv, i, rep_peer(d)).start()

    wait_in(grad_z.at[pl.ds(0, Z - 1)], z_recv)
    grad_out[mine] = jnp.sum(grad_z[...].astype(F32), axis=0).astype(BF16)

    def out_go(slot, blk, rep):
        remote(grad_out.at[mine], grad_out.at[mine], out_send, out_recv, blk, rep).start()

    group_loop(out_go)
    wait_in(score_all.at[pl.ds(0, ROWS - PIECE)], sa_recv)
    save_scores = pltpu.make_async_copy(score_all, scores_hbm, save_sem.at[0])
    save_scores.start()
    wait_in(grad_out.at[pl.ds(0, GROUPS - 1)], out_recv)
    grad_full[...] = grad_out[...].astype(F32).reshape(HID, FEAT)
    save_grad = pltpu.make_async_copy(grad_full, grad_hbm, save_sem.at[1])
    save_grad.start()

    for layer in range(2):
        wait_out(recv_far.at[layer, pl.ds(0, N - 1)], far_send.at[layer])
        wait_out(relay.at[layer], relay_send.at[layer])
        wait_out(blocks.at[layer, pl.ds(0, 3)], block_send.at[layer])
        wait_out(relay.at[layer, pl.ds(0, 5)], block_send.at[layer])
        twice = jnp.logical_or(r == 1, r == 5)
        never = jnp.logical_or(r == 0, r == 4)
        pl.when(jnp.logical_not(twice))(lambda: wait_out(relay.at[layer, 0], block_send.at[layer]))
        pl.when(never)(lambda: wait_out(relay.at[layer, 0], block_send.at[layer]))
    wait_out(shares.at[pl.ds(0, R - 1)], cut_send)
    wait_out(whole.at[pl.ds(0, ROWS - PIECE)], whole_send)
    wait_out(score_in.at[pl.ds(0, R - 1)], sc_send)
    wait_out(score_all.at[pl.ds(0, ROWS - PIECE)], sa_send)
    wait_out(grad_in.at[pl.ds(0, GROUPS - 1)], grad_send)
    wait_out(grad_z.at[pl.ds(0, Z - 1)], z_send)
    wait_out(grad_out.at[pl.ds(0, GROUPS - 1)], out_send)
    save_scores.wait()
    save_grad.wait()


def per_device(features, band_weight, far_weight, send_rows, layer_one, layer_two, cotangent):
    dma, regular, vmem = pltpu.SemaphoreType.DMA, pltpu.SemaphoreType.REGULAR, pltpu.VMEM
    anywhere = pl.BlockSpec(memory_space=pl.ANY)
    here = pl.BlockSpec(memory_space=pltpu.VMEM)
    scratch = [
        vmem((ROWS, FEAT), BF16),
        vmem((ROWS, STEPS * ROWS), BF16),
        vmem((ROWS, SLOTS), BF16),
        vmem((FEAT, HID), BF16),
        vmem((HID, FEAT), BF16),
        vmem((ROWS, FEAT), BF16),
        vmem((SLOTS, ROWS), BF16),
        vmem((ROWS, HID), F32),
        vmem((STEPS, ROWS, 2 * FEAT), BF16),
        vmem((SLOTS, 2 * FEAT), BF16),
        vmem((HID, 2 * FEAT), F32),
        vmem((HID, FEAT), F32),
        vmem((2, N, 2, FEAT), BF16),
        vmem((2, N, 2, FEAT), BF16),
        vmem((2, R, PIECE, FEAT), BF16),
        vmem((2, STEPS, ROWS, FEAT), BF16),
        vmem((ROWS, FEAT), BF16),
        vmem((R, PIECE, FEAT), BF16),
        vmem((R, PIECE, FEAT), BF16),
        vmem((GROUPS, SHARE, FEAT), BF16),
        vmem((GROUPS, SHARE, FEAT), BF16),
        vmem((Z, SHARE, FEAT), BF16),
        vmem((GROUPS, SHARE, FEAT), BF16),
        vmem((R, PIECE, FEAT), BF16),
        vmem((R, PIECE, FEAT), BF16),
        vmem((R, PIECE, FEAT), F32),
        vmem((ROWS, FEAT), BF16),
        dma((6,)), dma((2,)), regular, regular,
        dma((2,)), dma((2,)), dma((2,)), dma((2,)), dma((2, R)), dma((2,)), dma((2, STEPS)),
        dma, dma, dma, dma,
        dma, dma, dma, dma, dma, dma,
        dma, dma, dma, dma,
    ]
    return pl.pallas_call(
        kernel,
        out_shape=(jax.ShapeDtypeStruct((ROWS, FEAT), BF16), jax.ShapeDtypeStruct((HID, FEAT), F32)),
        in_specs=[anywhere, anywhere, anywhere, here, anywhere, anywhere, anywhere],
        out_specs=(anywhere, anywhere),
        scratch_shapes=scratch,
        name="graph",
        compiler_params=pltpu.CompilerParams(collective_id=0, has_side_effects=True, vmem_limit_bytes=60 << 20),
    )(features, band_weight, far_weight, send_rows.reshape(1, SLOTS), layer_one, layer_two, cotangent)


def solution(mesh):
    return jax.shard_map(
        per_device,
        mesh=mesh,
        in_specs=(
            P("blk", None),
            P("blk", "rep"),
            P("blk", "rep"),
            P("blk", "rep", None),
            P(),
            P(),
            P("blk", None),
        ),
        out_specs=(P("blk", None), P()),
        check_vma=False,
    )
```
